32 devices in a mesh: grp: 2 (over y), term: 4 (over z), sec: 2 (over x), sub: 2 (over core).
Axes of the slice: x: 2, y: 2, z: 4, core: 2. Of those that a mesh axis runs over, the one named last changes fastest.
Arguments:
- wavefunction: float32 [8, 8, 256, 256], P(('grp', 'sec'), None, None, 'sub'), parts along dimension 0, may hold values from -6 to 6
- left_operators: float32 [12, 8, 256, 256], P('term', ('grp', 'sec')), parts along dimension 1, may hold values from -0.5 to 0.5
- right_operators: float32 [12, 8, 256, 256], P('term', ('grp', 'sec'), 'sub'), parts along dimension 1, may hold values from -0.109375 to 0.109375
- source_sectors: int32 [12, 8], P('term', ('grp', 'sec')), parts along dimension 1, may hold values from 0 to 3, as said below
Outputs:
- sigma_blocks: float32 [8, 8, 256, 256], P(('grp', 'sec'), None, 'term', 'sub'), parts along dimension 0
The draws below stay inside these ranges and needn't reach their ends.
There are 2 independent parts, one for each index of `grp`. The reference program is written for one: setup_inputs(seed, part) draws one part's arguments, and reference() takes and returns one part's arrays. A program takes and returns all parts, laid end to end along the dimension named above; each array names one. Nothing has to cross between parts.
Inputs may be any that keep to these rules, and one draw needn't show every extreme that they name: source_sectors[t, s] differs from s by at most 1.
All inputs are finite; a program needn't handle non-finite values.
Results may differ from the reference program's by a relative error of at most 0.0003.
Values sent between devices are 32-bit elements; how exact they have to be, the bound alone decides.
No kernel may reach another device: no remote copies, remote signals or barrier semaphores. Data moves between devices by JAX's collectives and lax.ppermute only.
A program may use at most 64 MiB of HBM per device.

```python
import jax
import jax.numpy as jnp
from jax import lax

LEFT_DIM = 256
RIGHT_DIM = 256
SEC_DEV = 2
VECTORS = 8
REACH = 1
TERMS = 12
SECTORS = 4


def draw_source_sectors(key, part):
    key = jax.random.fold_in(key, 7)
    shifts = jax.random.randint(key, (TERMS, SECTORS), -REACH, REACH + 1)
    term_ids = jnp.arange(TERMS)[:, None]
    sector_ids = jnp.arange(SECTORS)[None, :]
    position = sector_ids % SEC_DEV
    shifts = jnp.where((term_ids % 2 == 0) & (position == 0), -REACH, shifts)
    shifts = jnp.where((term_ids % 2 == 1) & (position == SEC_DEV - 1), REACH, shifts)
    return jnp.clip(sector_ids + shifts, 0, SECTORS - 1).astype(jnp.int32)


def spiked(drawn, key, source, target, shards_of, factor):
    owner, partner = [(jnp.arange(drawn.shape[axis_at]) // (drawn.shape[axis_at] // shards_of)).reshape([-1 if axis == axis_at else 1 for axis in range(drawn.ndim)]) for axis_at in (source, target)]
    chosen = jax.random.permutation(key, shards_of)[partner]
    strong = (owner == chosen) | (owner == (partner + shards_of // 2) % shards_of)
    return jnp.where(strong, factor * drawn, drawn)


def block_scale(own_key, dims, shards, smallest, top_value):
    factor_of, own = 1.0, jax.random.fold_in(own_key, 6)
    for axis_at, parts in shards:
        steps = jnp.exp(jax.random.uniform(jax.random.fold_in(own, axis_at), (parts,), jnp.float32, smallest / len(shards), top_value / len(shards)))
        factor_of = factor_of * jnp.repeat(steps, dims[axis_at] // parts).reshape([-1 if axis == axis_at else 1 for axis in range(len(dims))])
    return factor_of


def noise(rng, shape, scale, bound, split=(), kind=jnp.bfloat16):
    values = scale * jax.random.normal(rng, shape, jnp.float32)
    if split:
        values = values * block_scale(rng, shape, split, -0.22, 0.18)
    return jnp.clip(values, -bound, bound).astype(kind)


def bell_draw_with(key, dims, spread, limit, shards, heavy, kind=jnp.bfloat16):
    array = spread * jax.random.normal(key, dims, jnp.float32)
    if shards:
        array = array * block_scale(key, dims, shards, -0.22, 0.18)
    return jnp.clip(spiked(array, jax.random.fold_in(key, 3), *heavy), -limit, limit).astype(kind)


def setup_inputs(seed: int = 0, part: int = 0) -> dict:
    arg_keys = jax.random.split(jax.random.key(seed), 5)
    own_keys = jax.random.split(jax.random.fold_in(arg_keys[4], part), 5)
    return {
        "wavefunction": noise(own_keys[0], (SECTORS, VECTORS, LEFT_DIM, RIGHT_DIM), 1.0, 6.0, ((0, 2), (3, 2)), jnp.float32),
        "left_operators": bell_draw_with(own_keys[1], (TERMS, SECTORS, LEFT_DIM, LEFT_DIM), LEFT_DIM ** -0.5, 0.5, ((0, 4), (1, 2)), (0, 2, 4, 2.0), jnp.float32),
        "right_operators": noise(own_keys[2], (TERMS, SECTORS, RIGHT_DIM, RIGHT_DIM), (RIGHT_DIM * TERMS) ** -0.5, 0.109375, ((0, 4), (1, 2), (2, 2)), jnp.float32),
        "source_sectors": draw_source_sectors(jax.random.fold_in(jax.random.fold_in(arg_keys[4], part), 71), part),
    }


def reference(wavefunction, left_operators, right_operators, source_sectors):
    highest = lax.Precision.HIGHEST

    def one_term(running, items):
        left_block, right_block, source_row = items
        picked = jnp.take(wavefunction, source_row.astype(jnp.int32), axis=0)
        middle = jnp.einsum("sij,svjk->svik", left_block, picked, precision=highest)
        update = jnp.einsum("svik,skl->svil", middle, right_block, precision=highest)
        return running + update, None

    initial = jnp.zeros(wavefunction.shape, jnp.float32)
    running, unused = lax.scan(one_term, initial, (left_operators, right_operators, source_sectors))
    return running
```

```python
import functools

import jax
import jax.numpy as jnp
from jax import lax
from jax.experimental import pallas as pl
from jax.experimental.pallas import tpu as pltpu
from jax.sharding import PartitionSpec as P

CHUNKS = 2


def halving_order(peers):
    bits = peers.bit_length() - 1
    assert peers == 1 << bits
    return sorted(range(peers), key=lambda m: -sum(((m >> b) & 1) << (bits - 1 - b) for b in range(bits)))


def halves(value):
    high = value.astype(jnp.bfloat16)
    return high, (value - high.astype(jnp.float32)).astype(jnp.bfloat16)


def chunk_kernel(order, terms, with_halo, scalars, *refs):
    left, right_own, right_other, psi = refs[:4]
    halo = refs[4] if with_halo else None
    own, other, left_cat, right_cat, psi_cat, mid_cat = refs[4 + with_halo:]
    rows, depth = left.shape[2], left.shape[3]
    width = psi.shape[3]
    piece = rows // len(order)
    columns = right_own.shape[3]

    @pl.when(pl.program_id(0) == 0)
    def _():
        for t in range(terms):
            ordered = [left[t, 0, pl.ds(pl.multiple_of((scalars[1] ^ m) * piece, piece), piece), :] for m in order]
            high, low = halves(jnp.concatenate(ordered, axis=0))
            left_cat[t, :, 0:depth] = high
            left_cat[t, :, depth:2 * depth] = high
            left_cat[t, :, 2 * depth:3 * depth] = low
            for at, ref in ((0, right_own), (columns, right_other)):
                high, low = halves(ref[t, 0])
                start = t * 3 * width
                right_cat[start:start + width, at:at + columns] = high
                right_cat[start + width:start + 2 * width, at:at + columns] = high
                right_cat[start + 2 * width:start + 3 * width, at:at + columns] = low

    for source in range(2 + with_halo):
        for v in range(2):
            high, low = halves(psi[source, v] if source < 2 else halo[v])
            psi_cat[source, 0:depth, v * width:(v + 1) * width] = high
            psi_cat[source, depth:2 * depth, v * width:(v + 1) * width] = low
            psi_cat[source, 2 * depth:3 * depth, v * width:(v + 1) * width] = high
    for t in range(terms):
        mid = jnp.dot(left_cat[t], psi_cat[scalars[3 + t]], preferred_element_type=jnp.float32)
        high, low = halves(mid)
        for v in range(2):
            start = t * 3 * width
            mid_cat[v * rows:(v + 1) * rows, start:start + width] = high[:, v * width:(v + 1) * width]
            mid_cat[v * rows:(v + 1) * rows, start + width:start + 2 * width] = low[:, v * width:(v + 1) * width]
            mid_cat[v * rows:(v + 1) * rows, start + 2 * width:start + 3 * width] = high[:, v * width:(v + 1) * width]
    total = jnp.dot(mid_cat[...], right_cat[...], preferred_element_type=jnp.float32)
    for v in range(2):
        for p in range(len(order)):
            start = v * rows + p * piece
            own[p, v] = total[start:start + piece, 0:columns]
            other[p, v] = total[start:start + piece, columns:2 * columns]


def chunk(scalars, left, right, psi, halo, first, count, order):
    terms, _, rows, depth = left.shape
    width, columns = psi.shape[3], right.shape[3] // 2
    piece = rows // len(order)
    lead = first // 2
    with_halo = halo is not None
    in_specs = [
        pl.BlockSpec((terms, 1, rows, depth), lambda i, s: (0, s[0], 0, 0)),
        pl.BlockSpec((terms, 1, width, columns), lambda i, s: (0, s[0], 0, s[2])),
        pl.BlockSpec((terms, 1, width, columns), lambda i, s: (0, s[0], 0, 1 - s[2])),
        pl.BlockSpec((2, 2, depth, width), lambda i, s: (0, lead + i, 0, 0)),
    ]
    args = [left, right, right, psi]
    if with_halo:
        in_specs.append(pl.BlockSpec((2, depth, width), lambda i, s: (i, 0, 0)))
        args.append(halo)
    out = jax.ShapeDtypeStruct((len(order), count, piece, columns), jnp.float32)
    out_spec = pl.BlockSpec((len(order), 2, piece, columns), lambda i, s: (0, i, 0, 0))
    flops = 2 * 3 * terms * count * rows * width * (depth + 2 * columns)
    return pl.pallas_call(
        functools.partial(chunk_kernel, order, terms, with_halo),
        out_shape=(out, out),
        grid_spec=pltpu.PrefetchScalarGridSpec(
            num_scalar_prefetch=1,
            grid=(count // 2,),
            in_specs=in_specs,
            out_specs=(out_spec, out_spec),
            scratch_shapes=[
                pltpu.VMEM((terms, rows, 3 * depth), jnp.bfloat16),
                pltpu.VMEM((terms * 3 * width, 2 * columns), jnp.bfloat16),
                pltpu.VMEM((2 + with_halo, 3 * depth, 2 * width), jnp.bfloat16),
                pltpu.VMEM((2 * rows, terms * 3 * width), jnp.bfloat16),
            ],
        ),
        compiler_params=pltpu.CompilerParams(vmem_limit_bytes=32 * 1024 * 1024),
        cost_estimate=pl.CostEstimate(flops=flops, bytes_accessed=8 * 1024 * 1024, transcendentals=0),
        name="terms_of_sector",
    )(scalars, *args)


def shards(wavefunction, left_operators, right_operators, source_sectors):
    sectors, vectors = wavefunction.shape[:2]
    assert sectors == 2
    peers, places = lax.axis_size("term"), lax.axis_size("sec")
    z, x, core = lax.axis_index("term"), lax.axis_index("sec"), lax.axis_index("sub")
    order = halving_order(peers)
    stages = [[(i, i ^ (1 << b)) for i in range(peers)] for b in range(peers.bit_length() - 1)]
    swap = [(0, 1), (1, 0)]
    relative = source_sectors - x * sectors
    picks = jnp.where((relative >= 0) & (relative < sectors), relative, 2)
    count = vectors // CHUNKS

    targets = (x, 1 - x) if places == 2 else (jnp.int32(0), jnp.int32(1))

    def halo_of(which, first):
        if places == 2:
            if which == 0:
                return None
            edge, perm = targets[1], swap
        elif which == 0:
            edge, perm = jnp.int32(1), [(i, i + 1) for i in range(places - 1)]
        else:
            edge, perm = jnp.int32(0), [(i + 1, i) for i in range(places - 1)]
        sent = lax.dynamic_slice(wavefunction, (edge, first, 0, 0), (1, count) + wavefunction.shape[2:])[0]
        return lax.ppermute(sent, "sec", perm)

    work = [(which, first) for which in range(2) for first in range(0, vectors, count)]
    halos = {item: halo_of(*item) for item in work}
    done = {}
    for which, first in work:
        target = targets[which]
        scalars = jnp.concatenate([jnp.stack([target, z, core]), lax.dynamic_index_in_dim(picks, target, 1, keepdims=False)])
        own, other = chunk(scalars, left_operators, right_operators, wavefunction, halos[which, first], first, count, order)
        addends = [own, lax.ppermute(other, "sub", swap)]
        for perm in stages:
            half = addends[0].shape[0] // 2
            sent = sum(a[:half] for a in addends)
            addends = [a[half:] for a in addends] + [lax.ppermute(sent, "term", perm)]
        done[which, first] = sum(a[0] for a in addends)
    outs = [jnp.concatenate([done[which, first] for first in range(0, vectors, count)], axis=0) for which in range(2)]
    if places == 2:
        outs = [jnp.where(x == 0, outs[0], outs[1]), jnp.where(x == 0, outs[1], outs[0])]
    return jnp.stack(outs)


def solution(mesh):
    in_specs = (
        P(("grp", "sec"), None, None, "sub"),
        P("term", ("grp", "sec"), None, None),
        P("term", ("grp", "sec"), "sub", None),
        P("term", ("grp", "sec")),
    )
    out_specs = P(("grp", "sec"), None, "term", "sub")
    return jax.shard_map(shards, mesh=mesh, in_specs=in_specs, out_specs=out_specs, check_vma=False)
```

```python
import functools

import jax
import jax.numpy as jnp
from jax import lax
from jax.experimental import pallas as pl
from jax.experimental.pallas import tpu as pltpu
from jax.sharding import PartitionSpec as P

CHUNKS = 2
ANY = pl.BlockSpec(memory_space=pl.ANY)
VMEM = pl.BlockSpec(memory_space=pltpu.VMEM)


def halving_order(peers):
    bits = peers.bit_length() - 1
    assert peers == 1 << bits
    return sorted(range(peers), key=lambda m: -sum(((m >> b) & 1) << (bits - 1 - b) for b in range(bits)))


def halves(value):
    high = value.astype(jnp.bfloat16)
    return high, (value - high.astype(jnp.float32)).astype(jnp.bfloat16)


def pinned(space, *values):
    return [pltpu.with_memory_space_constraint(value, space) for value in values]


def edge_kernel(count, scalars, psi, earlier, *refs):
    edges, sem = refs[:-1], refs[-1]
    copies = [
        pltpu.make_async_copy(psi.at[scalars[0], pl.ds(c * count, count)], edge, sem.at[c]) for c, edge in enumerate(edges)
    ]
    for copy in copies:
        copy.start()
    for copy in copies:
        copy.wait()


def edges_of(sector, psi, count, earlier):
    chunks = psi.shape[1] // count
    edge = jax.ShapeDtypeStruct((count,) + psi.shape[2:], psi.dtype)
    return pl.pallas_call(
        functools.partial(edge_kernel, count),
        out_shape=[edge] * chunks,
        in_specs=[pl.BlockSpec(memory_space=pltpu.SMEM), pl.BlockSpec(memory_space=pltpu.HBM), ANY],
        out_specs=[VMEM] * chunks,
        scratch_shapes=[pltpu.SemaphoreType.DMA((chunks,))],
        compiler_params=pltpu.CompilerParams(vmem_limit_bytes=1024 * 1024),
        name="edges",
    )(jnp.reshape(sector, (1,)), *pinned(pltpu.HBM, psi), earlier)


def relay_kernel(value, earlier, out):
    pass


def relay(value, earlier):
    return pl.pallas_call(
        relay_kernel,
        out_shape=jax.ShapeDtypeStruct(value.shape, value.dtype),
        in_specs=[ANY, ANY],
        out_specs=ANY,
        input_output_aliases={0: 0},
        compiler_params=pltpu.CompilerParams(vmem_limit_bytes=1024 * 1024),
        name="relay",
    )(value, earlier)


def stage_kernel(order, scalars, left, left_cat):
    terms, rows, depth = left.shape[0], left.shape[2], left.shape[3]
    piece = rows // len(order)
    for t in range(terms):
        ordered = [left[t, 0, pl.ds(pl.multiple_of((scalars[0] ^ m) * piece, piece), piece), :] for m in order]
        high, low = halves(jnp.concatenate(ordered, axis=0))
        start = t * 3 * depth
        left_cat[0, :, start:start + depth] = high
        left_cat[0, :, start + depth:start + 2 * depth] = high
        left_cat[0, :, start + 2 * depth:start + 3 * depth] = low


def staged(place, left, order):
    terms, sectors, rows, depth = left.shape
    return pl.pallas_call(
        functools.partial(stage_kernel, order),
        out_shape=jax.ShapeDtypeStruct((sectors, rows, terms * 3 * depth), jnp.bfloat16),
        grid_spec=pltpu.PrefetchScalarGridSpec(
            num_scalar_prefetch=1,
            grid=(sectors,),
            in_specs=[pl.BlockSpec((terms, 1, rows, depth), lambda i, s: (0, i, 0, 0))],
            out_specs=pl.BlockSpec((1, rows, terms * 3 * depth), lambda i, s: (i, 0, 0)),
        ),
        compiler_params=pltpu.CompilerParams(vmem_limit_bytes=16 * 1024 * 1024),
        name="stage",
    )(jnp.reshape(place, (1,)), *pinned(pltpu.HBM, left))


def summed(addends, size, earlier):
    def kernel(*refs):
        pieces = [ref[start:start + size] for ref, (array, start) in zip(refs, addends)]
        refs[-1][...] = functools.reduce(lambda a, b: a + b, pieces)

    return pl.pallas_call(
        kernel,
        out_shape=jax.ShapeDtypeStruct((size,) + addends[0][0].shape[1:], jnp.float32),
        in_specs=[VMEM] * len(addends) + [ANY] * len(earlier),
        out_specs=VMEM,
        compiler_params=pltpu.CompilerParams(vmem_limit_bytes=4 * 1024 * 1024),
        name="summed",
    )(*[array for array, start in addends], *earlier)


def gather_kernel(counts, scalars, *refs):
    out, at = refs[-1], 0
    for which, first, starts in counts:
        total = functools.reduce(lambda a, b: a + b, [ref[start] for ref, start in zip(refs[at:], starts)])
        out[scalars[which], first:first + total.shape[0]] = total
        at += len(starts)


def gathered(targets, items, shape):
    addends = [addend for item in items.values() for addend in item]

    return pl.pallas_call(
        functools.partial(gather_kernel, [(*item, [start for array, start in each]) for item, each in items.items()]),
        out_shape=jax.ShapeDtypeStruct(shape, jnp.float32),
        in_specs=[pl.BlockSpec(memory_space=pltpu.SMEM)] + [VMEM] * len(addends),
        out_specs=VMEM,
        compiler_params=pltpu.CompilerParams(vmem_limit_bytes=8 * 1024 * 1024),
        name="gathered",
    )(jnp.stack(targets), *[array for array, start in addends])


def chunk_kernel(order, terms, first, count, with_halo, scalars, left_cat, *refs):
    rights, psis, halos = refs[:2], refs[2:4], refs[4:4 + 2 * with_halo]
    sent, kept, left_in, right_in, psi_in, right_cat, psi_cat, mid_cat, sem = refs[-9:]
    depth, width = psis[0].shape[2:]
    columns = right_in.shape[3]
    piece = left_in.shape[0] // len(order)
    sources = 2 + with_halo
    target, here = scalars[0], pl.ds(pl.multiple_of(scalars[1] * columns, columns), columns)

    right_copies = [pltpu.make_async_copy(rights[at].at[:, target, :, here], right_in.at[at], sem.at[at]) for at in range(2)]
    psi_copies = {}
    for source in range(sources):
        for at in range(2):
            origin = psis[at].at[source, pl.ds(first, count)] if source < 2 else halos[at]
            psi_copies[source, at] = pltpu.make_async_copy(origin, psi_in.at[source, at], sem.at[2 + 2 * source + at])
    left_copy = pltpu.make_async_copy(left_cat.at[target], left_in, sem.at[2 + 2 * sources])
    for copy in right_copies + list(psi_copies.values()) + [left_copy]:
        copy.start()

    for at in range(2):
        right_copies[at].wait()
        for t in range(terms):
            high, low = halves(right_in[at, t])
            for again in (at * width, (at + 2) * width):
                right_cat[t, again:again + width, 0:columns] = high
                right_cat[t, again:again + width, columns:2 * columns] = low
    for source in range(sources):
        for at in range(2):
            psi_copies[source, at].wait()
            for v in range(count):
                high, low = halves(psi_in[source, at, v])
                psi_cat[source, v * depth:(v + 1) * depth, at * width:(at + 1) * width] = high
                psi_cat[source, v * depth:(v + 1) * depth, (2 + at) * width:(3 + at) * width] = low
    for t in range(terms):
        mid = jnp.dot(psi_cat[scalars[2 + t]], right_cat[t], preferred_element_type=jnp.float32)
        high, low = halves(mid[:, 0:columns] + mid[:, columns:2 * columns])
        for v in range(count):
            start = t * 3 * depth
            mid_cat[start:start + depth, v * columns:(v + 1) * columns] = high[v * depth:(v + 1) * depth]
            mid_cat[start + depth:start + 2 * depth, v * columns:(v + 1) * columns] = low[v * depth:(v + 1) * depth]
            mid_cat[start + 2 * depth:start + 3 * depth, v * columns:(v + 1) * columns] = high[v * depth:(v + 1) * depth]
    left_copy.wait()
    total = jnp.dot(left_in[...], mid_cat[...], preferred_element_type=jnp.float32)
    half = len(order) // 2
    for v in range(count):
        for p in range(len(order)):
            ref = sent if p < half else kept
            ref[p % half, v] = total[p * piece:(p + 1) * piece, v * columns:(v + 1) * columns]


def chunk(scalars, left_cat, rights, psis, halos, first, count, order, earlier=()):
    rows = left_cat.shape[1]
    depth, width = psis[0].shape[2:]
    terms, columns = rights[0].shape[0], rights[0].shape[3] // 2
    with_halo = halos is not None
    args = pinned(pltpu.HBM, left_cat, rights[0]) + [rights[1]] + pinned(pltpu.HBM, psis[0]) + [psis[1], *(halos or ()), *earlier]
    out = jax.ShapeDtypeStruct((len(order) // 2, count, rows // len(order), columns), jnp.float32)
    flops = 2 * 3 * terms * count * rows * columns * (depth + 2 * width)
    sources = 2 + with_halo
    return pl.pallas_call(
        functools.partial(chunk_kernel, order, terms, first, count, with_halo),
        out_shape=(out, out),
        in_specs=[pl.BlockSpec(memory_space=pltpu.SMEM)] + [ANY] * len(args),
        out_specs=(VMEM,) * 2,
        scratch_shapes=[
            pltpu.VMEM((rows, terms * 3 * depth), jnp.bfloat16),
            pltpu.VMEM((2, terms, width, columns), jnp.float32),
            pltpu.VMEM((sources, 2, count, depth, width), jnp.float32),
            pltpu.VMEM((terms, 4 * width, 2 * columns), jnp.bfloat16),
            pltpu.VMEM((sources, count * depth, 4 * width), jnp.bfloat16),
            pltpu.VMEM((terms * 3 * depth, count * columns), jnp.bfloat16),
            pltpu.SemaphoreType.DMA((3 + 2 * sources,)),
        ],
        compiler_params=pltpu.CompilerParams(vmem_limit_bytes=20 * 1024 * 1024),
        cost_estimate=pl.CostEstimate(flops=flops, bytes_accessed=8 * 1024 * 1024, transcendentals=0),
        name="terms_of_sector",
    )(scalars, *args)


def shards(wavefunction, left_operators, right_operators, source_sectors):
    sectors, vectors = wavefunction.shape[:2]
    assert sectors == 2
    peers, places = lax.axis_size("term"), lax.axis_size("sec")
    z, x, core = lax.axis_index("term"), lax.axis_index("sec"), lax.axis_index("sub")
    order = halving_order(peers)
    stages = [[(i, i ^ (1 << b)) for i in range(peers)] for b in range(peers.bit_length() - 1)]
    swap = [(0, 1), (1, 0)]
    relative = source_sectors - x * sectors
    picks = jnp.where((relative >= 0) & (relative < sectors), relative, 2)
    count = vectors // CHUNKS
    psis = [wavefunction, lax.ppermute(wavefunction, "sub", swap)]
    rights = [right_operators, lax.ppermute(right_operators, "sub", swap)]
    left_cat = staged(z, left_operators, order)

    targets = (x, 1 - x) if places == 2 else (jnp.int32(0), jnp.int32(1))

    if places == 2:
        ways = [None, (targets[1], swap)]
    else:
        up = [(i, i + 1) for i in range(places - 1)]
        ways = [(jnp.int32(1), up), (jnp.int32(0), [(j, i) for i, j in up])]
    halos = {}
    for which in range(2):
        if ways[which] is not None:
            edges = edges_of(ways[which][0], wavefunction, count, left_cat)
            for c, edge in enumerate(edges):
                halos[which, c * count] = lax.ppermute(edge, "sec", ways[which][1])

    def compute(item, earlier):
        which, first = item
        sources = lax.dynamic_index_in_dim(picks, targets[which], 1, keepdims=False)
        both = None
        if item in halos:
            halo = halos[item] if earlier is None else relay(halos[item], earlier)
            both = [halo, lax.ppermute(halo, "sub", swap)]
        else:
            sources = jnp.minimum(sources, 1)
        scalars = jnp.concatenate([jnp.stack([targets[which], core]), sources])
        return chunk(scalars, left_cat, rights, psis, both, first, count, order, [] if earlier is None else [earlier])

    work = [(which, first) for which in range(2) for first in range(0, vectors, count)]
    parts, last, newest = {}, None, None
    for at in range(len(work) + len(stages) - 1):
        if at < len(work):
            item = work[at]
            newest, kept = compute(item, last)
            parts[item] = [(kept, 0), (lax.ppermute(newest, "term", stages[0]), 0)]
        for stage in range(1, len(stages)):
            if 0 <= at - stage < len(work):
                item = work[at - stage]
                half = peers >> (stage + 1)
                behind = parts[work[at - stage - 1]][-1:] if at > stage else []
                last = summed(parts[item], half, [newest] + [array for array, start in behind])
                parts[item] = [(array, start + half) for array, start in parts[item]]
                parts[item].append((lax.ppermute(last, "term", stages[stage]), 0))
    return gathered(targets, parts, (sectors, vectors) + parts[work[0]][0][0].shape[2:])


def solution(mesh):
    in_specs = (
        P(("grp", "sec"), None, None, "sub"),
        P("term", ("grp", "sec"), None, None),
        P("term", ("grp", "sec"), "sub", None),
        P("term", ("grp", "sec")),
    )
    out_specs = P(("grp", "sec"), None, "term", "sub")
    return jax.shard_map(shards, mesh=mesh, in_specs=in_specs, out_specs=out_specs, check_vma=False)
```

```python
import functools

import jax
import jax.numpy as jnp
from jax import lax
from jax.experimental import pallas as pl
from jax.experimental.pallas import tpu as pltpu
from jax.sharding import PartitionSpec as P

CHUNKS = 2
ANY = pl.BlockSpec(memory_space=pl.ANY)
VMEM = pl.BlockSpec(memory_space=pltpu.VMEM)


def halving_order(peers):
    bits = peers.bit_length() - 1
    assert peers == 1 << bits
    return sorted(range(peers), key=lambda m: -sum(((m >> b) & 1) << (bits - 1 - b) for b in range(bits)))


def halves(value):
    high = value.astype(jnp.bfloat16)
    return high, (value - high.astype(jnp.float32)).astype(jnp.bfloat16)


def pinned(space, *values):
    return [pltpu.with_memory_space_constraint(value, space) for value in values]


def edge_kernel(first, scalars, psi, *refs):
    edge, sem = refs[-2:]
    copies = [pltpu.make_async_copy(psi.at[scalars[0], first + v], edge.at[v], sem.at[v]) for v in range(edge.shape[0])]
    for copy in copies:
        copy.start()
    for copy in copies:
        copy.wait()


def edge_of(sector, psi, first, count, *earlier):
    return pl.pallas_call(
        functools.partial(edge_kernel, first),
        out_shape=jax.ShapeDtypeStruct((count,) + psi.shape[2:], psi.dtype),
        in_specs=[pl.BlockSpec(memory_space=pltpu.SMEM), pl.BlockSpec(memory_space=pltpu.HBM)] + [ANY] * len(earlier),
        out_specs=VMEM,
        scratch_shapes=[pltpu.SemaphoreType.DMA((count,))],
        compiler_params=pltpu.CompilerParams(vmem_limit_bytes=1024 * 1024),
        cost_estimate=pl.CostEstimate(flops=1024, bytes_accessed=1024, transcendentals=0),
        name="edge",
    )(jnp.reshape(sector, (1,)), *pinned(pltpu.HBM, psi), *earlier)


def relay_kernel(*refs):
    pass


def relay(value, *earlier):
    return pl.pallas_call(
        relay_kernel,
        out_shape=jax.ShapeDtypeStruct(value.shape, value.dtype),
        in_specs=[ANY] * (1 + len(earlier)),
        out_specs=ANY,
        input_output_aliases={0: 0},
        compiler_params=pltpu.CompilerParams(vmem_limit_bytes=1024 * 1024),
        cost_estimate=pl.CostEstimate(flops=1024, bytes_accessed=1024, transcendentals=0),
        name="relay",
    )(value, *earlier)


def stage_kernel(order, scalars, left, earlier, left_cat):
    terms, rows, depth = left.shape[0], left.shape[2], left.shape[3]
    piece = rows // len(order)
    for t in range(terms):
        ordered = [left[t, 0, pl.ds(pl.multiple_of((scalars[0] ^ m) * piece, piece), piece), :] for m in order]
        high, low = halves(jnp.concatenate(ordered, axis=0))
        start = t * 3 * depth
        left_cat[0, :, start:start + depth] = high
        left_cat[0, :, start + depth:start + 2 * depth] = high
        left_cat[0, :, start + 2 * depth:start + 3 * depth] = low


def staged(place, left, order, earlier):
    terms, sectors, rows, depth = left.shape
    return pl.pallas_call(
        functools.partial(stage_kernel, order),
        out_shape=jax.ShapeDtypeStruct((sectors, rows, terms * 3 * depth), jnp.bfloat16),
        grid_spec=pltpu.PrefetchScalarGridSpec(
            num_scalar_prefetch=1,
            grid=(sectors,),
            in_specs=[pl.BlockSpec((terms, 1, rows, depth), lambda i, s: (0, i, 0, 0)), ANY],
            out_specs=pl.BlockSpec((1, rows, terms * 3 * depth), lambda i, s: (i, 0, 0)),
        ),
        compiler_params=pltpu.CompilerParams(vmem_limit_bytes=16 * 1024 * 1024),
        cost_estimate=pl.CostEstimate(flops=1024, bytes_accessed=1024, transcendentals=0),
        name="stage",
    )(jnp.reshape(place, (1,)), *pinned(pltpu.HBM, left), earlier)


def summed(addends, size, earlier):
    def kernel(*refs):
        pieces = [ref[start:start + size] for ref, (array, start) in zip(refs, addends)]
        refs[-1][...] = functools.reduce(lambda a, b: a + b, pieces)

    return pl.pallas_call(
        kernel,
        out_shape=jax.ShapeDtypeStruct((size,) + addends[0][0].shape[1:], jnp.float32),
        in_specs=[VMEM] * len(addends) + [ANY] * len(earlier),
        out_specs=VMEM,
        compiler_params=pltpu.CompilerParams(vmem_limit_bytes=4 * 1024 * 1024),
        cost_estimate=pl.CostEstimate(flops=1024, bytes_accessed=1024, transcendentals=0),
        name="summed",
    )(*[array for array, start in addends], *earlier)


def gather_kernel(counts, scalars, *refs):
    out, at = refs[-1], 0
    for (which, first, _), starts in counts:
        total = functools.reduce(lambda a, b: a + b, [ref[start] for ref, start in zip(refs[at:], starts)])
        out[scalars[which], first:first + total.shape[0]] = total
        at += len(starts)


def gathered(targets, items, shape):
    addends = [addend for item in items.values() for addend in item]

    return pl.pallas_call(
        functools.partial(gather_kernel, [(item, [start for array, start in each]) for item, each in items.items()]),
        out_shape=jax.ShapeDtypeStruct(shape, jnp.float32),
        in_specs=[pl.BlockSpec(memory_space=pltpu.SMEM)] + [VMEM] * len(addends),
        out_specs=VMEM,
        compiler_params=pltpu.CompilerParams(vmem_limit_bytes=8 * 1024 * 1024),
        cost_estimate=pl.CostEstimate(flops=1024, bytes_accessed=1024, transcendentals=0),
        name="gathered",
    )(jnp.stack(targets), *[array for array, start in addends])


def chunk_kernel(order, terms, first, count, with_halo, scalars, left_cat, *refs):
    rights, psis, halos = refs[:2], refs[2:4], refs[4:4 + with_halo]
    sent, kept, left_in, right_in, psi_in, right_cat, psi_cat, mid_cat, sem = refs[-9:]
    depth, width = psis[0].shape[2:]
    columns = right_in.shape[3]
    piece = left_in.shape[0] // len(order)
    sources = 2 + (with_halo > 0)
    target, here = scalars[0], pl.ds(pl.multiple_of(scalars[1] * columns, columns), columns)

    right_copies = [pltpu.make_async_copy(rights[at].at[:, target, :, here], right_in.at[at], sem.at[at]) for at in range(2)]
    psi_copies = {}
    for source in range(sources):
        for at in range(2):
            place = psi_in.at[source, at]
            if source < 2:
                copies = [(psis[at].at[source, pl.ds(first, count)], place)]
            elif at == 0:
                copies = [(halos[0], place)]
            else:
                size = count // (with_halo - 1)
                copies = [(ref, place.at[pl.ds(v * size, size)]) for v, ref in enumerate(halos[1:])]
            psi_copies[source, at] = [
                pltpu.make_async_copy(*copy, sem.at[3 + 2 * source + at + v]) for v, copy in enumerate(copies)
            ]
    left_copy = pltpu.make_async_copy(left_cat.at[target], left_in, sem.at[2])
    for copy in right_copies + sum(psi_copies.values(), []) + [left_copy]:
        copy.start()

    for at in range(2):
        right_copies[at].wait()
        for t in range(terms):
            high, low = halves(right_in[at, t])
            for again in (at * width, (at + 2) * width):
                right_cat[t, again:again + width, 0:columns] = high
                right_cat[t, again:again + width, columns:2 * columns] = low
    for source in range(sources):
        for at in range(2):
            for copy in psi_copies[source, at]:
                copy.wait()
            for v in range(count):
                high, low = halves(psi_in[source, at, v])
                psi_cat[source, v * depth:(v + 1) * depth, at * width:(at + 1) * width] = high
                psi_cat[source, v * depth:(v + 1) * depth, (2 + at) * width:(3 + at) * width] = low
    for t in range(terms):
        mid = jnp.dot(psi_cat[scalars[2 + t]], right_cat[t], preferred_element_type=jnp.float32)
        high, low = halves(mid[:, 0:columns] + mid[:, columns:2 * columns])
        for v in range(count):
            start = t * 3 * depth
            mid_cat[start:start + depth, v * columns:(v + 1) * columns] = high[v * depth:(v + 1) * depth]
            mid_cat[start + depth:start + 2 * depth, v * columns:(v + 1) * columns] = low[v * depth:(v + 1) * depth]
            mid_cat[start + 2 * depth:start + 3 * depth, v * columns:(v + 1) * columns] = high[v * depth:(v + 1) * depth]
    left_copy.wait()
    total = jnp.dot(left_in[...], mid_cat[...], preferred_element_type=jnp.float32)
    half = len(order) // 2
    for v in range(count):
        for p in range(len(order)):
            ref = sent if p < half else kept
            ref[p % half, v] = total[p * piece:(p + 1) * piece, v * columns:(v + 1) * columns]


def chunk(scalars, left_cat, rights, psis, halos, first, count, order, earlier=()):
    rows = left_cat.shape[1]
    depth, width = psis[0].shape[2:]
    terms, columns = rights[0].shape[0], rights[0].shape[3] // 2
    with_halo = len(halos or ())
    args = pinned(pltpu.HBM, left_cat, rights[0]) + [rights[1]] + pinned(pltpu.HBM, psis[0]) + [psis[1], *(halos or ()), *earlier]
    out = jax.ShapeDtypeStruct((len(order) // 2, count, rows // len(order), columns), jnp.float32)
    flops = 2 * 3 * terms * count * rows * columns * (depth + 2 * width)
    sources = 2 + (with_halo > 0)
    return pl.pallas_call(
        functools.partial(chunk_kernel, order, terms, first, count, with_halo),
        out_shape=(out, out),
        in_specs=[pl.BlockSpec(memory_space=pltpu.SMEM)] + [ANY] * len(args),
        out_specs=(VMEM,) * 2,
        scratch_shapes=[
            pltpu.VMEM((rows, terms * 3 * depth), jnp.bfloat16),
            pltpu.VMEM((2, terms, width, columns), jnp.float32),
            pltpu.VMEM((sources, 2, count, depth, width), jnp.float32),
            pltpu.VMEM((terms, 4 * width, 2 * columns), jnp.bfloat16),
            pltpu.VMEM((sources, count * depth, 4 * width), jnp.bfloat16),
            pltpu.VMEM((terms * 3 * depth, count * columns), jnp.bfloat16),
            pltpu.SemaphoreType.DMA((3 + 2 * sources + with_halo,)),
        ],
        compiler_params=pltpu.CompilerParams(vmem_limit_bytes=20 * 1024 * 1024),
        cost_estimate=pl.CostEstimate(flops=1024, bytes_accessed=1024, transcendentals=0),
        name="terms_of_sector",
    )(scalars, *args)


def shards(wavefunction, left_operators, right_operators, source_sectors):
    sectors, vectors = wavefunction.shape[:2]
    assert sectors == 2
    peers, places = lax.axis_size("term"), lax.axis_size("sec")
    z, x, core = lax.axis_index("term"), lax.axis_index("sec"), lax.axis_index("sub")
    order = halving_order(peers)
    stages = [[(i, i ^ (1 << b)) for i in range(peers)] for b in range(peers.bit_length() - 1)]
    swap = [(0, 1), (1, 0)]
    relative = source_sectors - x * sectors
    picks = jnp.where((relative >= 0) & (relative < sectors), relative, 2)
    count = vectors // CHUNKS
    psis = [wavefunction, lax.ppermute(wavefunction, "sub", swap)]
    rights = [right_operators, lax.ppermute(right_operators, "sub", swap)]
    left_cat = None

    targets = (x, 1 - x) if places == 2 else (jnp.int32(0), jnp.int32(1))

    if places == 2:
        ways = [None, (targets[1], swap)]
    else:
        up = [(i, i + 1) for i in range(places - 1)]
        ways = [(jnp.int32(1), up), (jnp.int32(0), [(j, i) for i, j in up])]
    halos = {}
    for which in range(2):
        if ways[which] is not None:
            for first in range(0, vectors, count):
                edge = edge_of(ways[which][0], wavefunction, first, count, *([] if left_cat is None else [left_cat]))
                halos[which, first] = lax.ppermute(edge, "sec", ways[which][1])
                if left_cat is None:
                    left_cat = staged(z, left_operators, order, edge)

    def compute(item, earlier, tie):
        which, first, count = item
        sources = lax.dynamic_index_in_dim(picks, targets[which], 1, keepdims=False)
        both = None
        if (which, first) in halos:
            halo = relay(halos[which, first], *tie) if tie is not None else halos[which, first]
            both = [halo] + [lax.ppermute(halo[v:v + 1], "sub", swap) for v in range(0, count, 1)]
        else:
            sources = jnp.minimum(sources, 1)
        scalars = jnp.concatenate([jnp.stack([targets[which], core]), sources])
        return chunk(scalars, left_cat, rights, psis, both, first, count, order, earlier)

    work = [(which, first, count) for which in range(2) for first in range(0, vectors, count)]
    parts = {}

    def begin(item, earlier=(), tie=None):
        sent, kept = compute(item, list(earlier), tie)
        parts[item] = [(kept, 0), (lax.ppermute(sent, "term", stages[0]), 0)]
        return sent

    def proceed(item, stage, earlier=()):
        half = peers >> (stage + 1)
        sent = summed(parts[item], half, list(earlier))
        parts[item] = [(array, start + half) for array, start in parts[item]]
        parts[item].append((lax.ppermute(sent, "term", stages[stage]), 0))
        return sent

    late = range(1, len(stages))
    a1, a2, b1, b2 = work
    sent = begin(a1)
    sent = begin(a2)
    first = sent
    last = [proceed(a1, stage, [sent]) for stage in late][-1]
    sent = begin(b1, tie=[last])
    last = [proceed(a2, stage, [sent]) for stage in late][-1]
    sent = begin(b2, [parts[a1][-1][0]], tie=[last])
    for stage in late:
        proceed(b1, stage, [sent])
    for stage in late:
        proceed(b2, stage)
    return gathered(targets, parts, (sectors, vectors) + parts[work[0]][0][0].shape[2:])


def solution(mesh):
    in_specs = (
        P(("grp", "sec"), None, None, "sub"),
        P("term", ("grp", "sec"), None, None),
        P("term", ("grp", "sec"), "sub", None),
        P("term", ("grp", "sec")),
    )
    out_specs = P(("grp", "sec"), None, "term", "sub")
    return jax.shard_map(shards, mesh=mesh, in_specs=in_specs, out_specs=out_specs, check_vma=False)
```

```python
import functools

import jax
import jax.numpy as jnp
from jax import lax
from jax.experimental import pallas as pl
from jax.experimental.pallas import tpu as pltpu
from jax.sharding import PartitionSpec as P

ANY = pl.BlockSpec(memory_space=pl.ANY)
VMEM = pl.BlockSpec(memory_space=pltpu.VMEM)


def halving_order(peers):
    bits = peers.bit_length() - 1
    assert peers == 1 << bits
    return sorted(range(peers), key=lambda m: -sum(((m >> b) & 1) << (bits - 1 - b) for b in range(bits)))


def halves(value):
    high = value.astype(jnp.bfloat16)
    return high, (value - high.astype(jnp.float32)).astype(jnp.bfloat16)


def pinned(space, *values):
    return [pltpu.with_memory_space_constraint(value, space) for value in values]


def edge_kernel(first, scalars, psi, *refs):
    edge, sem = refs[-2:]
    copies = [pltpu.make_async_copy(psi.at[scalars[0], first + v], edge.at[v], sem.at[v]) for v in range(edge.shape[0])]
    for copy in copies:
        copy.start()
    for copy in copies:
        copy.wait()


def edge_of(sector, psi, first, count, *earlier):
    return pl.pallas_call(
        functools.partial(edge_kernel, first),
        out_shape=jax.ShapeDtypeStruct((count,) + psi.shape[2:], psi.dtype),
        in_specs=[pl.BlockSpec(memory_space=pltpu.SMEM), pl.BlockSpec(memory_space=pltpu.HBM)] + [ANY] * len(earlier),
        out_specs=VMEM,
        scratch_shapes=[pltpu.SemaphoreType.DMA((count,))],
        compiler_params=pltpu.CompilerParams(vmem_limit_bytes=1024 * 1024),
        cost_estimate=pl.CostEstimate(flops=1024, bytes_accessed=1024, transcendentals=0),
        name="edge",
    )(jnp.reshape(sector, (1,)), *pinned(pltpu.HBM, psi), *earlier)


def relay_kernel(*refs):
    pass


def relay(value, *earlier):
    return pl.pallas_call(
        relay_kernel,
        out_shape=jax.ShapeDtypeStruct(value.shape, value.dtype),
        in_specs=[ANY] * (1 + len(earlier)),
        out_specs=ANY,
        input_output_aliases={0: 0},
        compiler_params=pltpu.CompilerParams(vmem_limit_bytes=1024 * 1024),
        cost_estimate=pl.CostEstimate(flops=1024, bytes_accessed=1024, transcendentals=0),
        name="relay",
    )(value, *earlier)


def stage_kernel(order, scalars, left, earlier, left_cat):
    terms, rows, depth = left.shape[0], left.shape[2], left.shape[3]
    piece = rows // len(order)
    for t in range(terms):
        ordered = [left[t, 0, pl.ds(pl.multiple_of((scalars[0] ^ m) * piece, piece), piece), :] for m in order]
        high, low = halves(jnp.concatenate(ordered, axis=0))
        start = t * 3 * depth
        left_cat[0, :, start:start + depth] = high
        left_cat[0, :, start + depth:start + 2 * depth] = high
        left_cat[0, :, start + 2 * depth:start + 3 * depth] = low


def staged(place, left, order, earlier):
    terms, sectors, rows, depth = left.shape
    return pl.pallas_call(
        functools.partial(stage_kernel, order),
        out_shape=jax.ShapeDtypeStruct((sectors, rows, terms * 3 * depth), jnp.bfloat16),
        grid_spec=pltpu.PrefetchScalarGridSpec(
            num_scalar_prefetch=1,
            grid=(sectors,),
            in_specs=[pl.BlockSpec((terms, 1, rows, depth), lambda i, s: (0, i, 0, 0)), ANY],
            out_specs=pl.BlockSpec((1, rows, terms * 3 * depth), lambda i, s: (i, 0, 0)),
        ),
        compiler_params=pltpu.CompilerParams(vmem_limit_bytes=16 * 1024 * 1024),
        cost_estimate=pl.CostEstimate(flops=1024, bytes_accessed=1024, transcendentals=0),
        name="stage",
    )(jnp.reshape(place, (1,)), *pinned(pltpu.HBM, left), earlier)


def summed(addends, size, earlier):
    def kernel(*refs):
        pieces = [ref[start:start + size] for ref, (array, start) in zip(refs, addends)]
        refs[-1][...] = functools.reduce(lambda a, b: a + b, pieces)

    return pl.pallas_call(
        kernel,
        out_shape=jax.ShapeDtypeStruct((size,) + addends[0][0].shape[1:], jnp.float32),
        in_specs=[VMEM] * len(addends) + [ANY] * len(earlier),
        out_specs=VMEM,
        compiler_params=pltpu.CompilerParams(vmem_limit_bytes=4 * 1024 * 1024),
        cost_estimate=pl.CostEstimate(flops=1024, bytes_accessed=1024, transcendentals=0),
        name="summed",
    )(*[array for array, start in addends], *earlier)


def gather_kernel(counts, scalars, *refs):
    out, at = refs[-1], 0
    for (which, first, _), starts in counts:
        total = functools.reduce(lambda a, b: a + b, [ref[start] for ref, start in zip(refs[at:], starts)])
        out[scalars[which], first:first + total.shape[0]] = total
        at += len(starts)


def gathered(targets, items, shape):
    addends = [addend for item in items.values() for addend in item]

    return pl.pallas_call(
        functools.partial(gather_kernel, [(item, [start for array, start in each]) for item, each in items.items()]),
        out_shape=jax.ShapeDtypeStruct(shape, jnp.float32),
        in_specs=[pl.BlockSpec(memory_space=pltpu.SMEM)] + [VMEM] * len(addends),
        out_specs=VMEM,
        compiler_params=pltpu.CompilerParams(vmem_limit_bytes=8 * 1024 * 1024),
        cost_estimate=pl.CostEstimate(flops=1024, bytes_accessed=1024, transcendentals=0),
        name="gathered",
    )(jnp.stack(targets), *[array for array, start in addends])


def chunk_kernel(order, terms, first, count, with_halo, scalars, left_cat, *refs):
    rights, psis, halos = refs[:2], refs[2:4], refs[4:4 + with_halo]
    sent, kept, left_in, right_in, psi_in, right_cat, psi_cat, mid_cat, sem = refs[-9:]
    depth, width = psis[0].shape[2:]
    columns = right_in.shape[3]
    piece = left_in.shape[0] // len(order)
    sources = 2 + (with_halo > 0)
    target, here = scalars[0], pl.ds(pl.multiple_of(scalars[1] * columns, columns), columns)

    right_copies = [pltpu.make_async_copy(rights[at].at[:, target, :, here], right_in.at[at], sem.at[at]) for at in range(2)]
    psi_copies = {}
    for source in range(sources):
        for at in range(2):
            place = psi_in.at[source, at]
            if source < 2:
                copies = [(psis[at].at[source, pl.ds(first, count)], place)]
            elif at == 0:
                copies = [(halos[0], place)]
            else:
                size = count // (with_halo - 1)
                copies = [(ref, place.at[pl.ds(v * size, size)]) for v, ref in enumerate(halos[1:])]
            psi_copies[source, at] = [
                pltpu.make_async_copy(*copy, sem.at[3 + 2 * source + at + v]) for v, copy in enumerate(copies)
            ]
    left_copy = pltpu.make_async_copy(left_cat.at[target], left_in, sem.at[2])
    for copy in right_copies + sum(psi_copies.values(), []) + [left_copy]:
        copy.start()

    for at in range(2):
        right_copies[at].wait()
        for t in range(terms):
            high, low = halves(right_in[at, t])
            for again in (at * width, (at + 2) * width):
                right_cat[t, again:again + width, 0:columns] = high
                right_cat[t, again:again + width, columns:2 * columns] = low
    for source in range(sources):
        for at in range(2):
            for copy in psi_copies[source, at]:
                copy.wait()
            for v in range(count):
                high, low = halves(psi_in[source, at, v])
                psi_cat[source, v * depth:(v + 1) * depth, at * width:(at + 1) * width] = high
                psi_cat[source, v * depth:(v + 1) * depth, (2 + at) * width:(3 + at) * width] = low
    for t in range(terms):
        mid = jnp.dot(psi_cat[scalars[2 + t]], right_cat[t], preferred_element_type=jnp.float32)
        high, low = halves(mid[:, 0:columns] + mid[:, columns:2 * columns])
        for v in range(count):
            start = t * 3 * depth
            mid_cat[start:start + depth, v * columns:(v + 1) * columns] = high[v * depth:(v + 1) * depth]
            mid_cat[start + depth:start + 2 * depth, v * columns:(v + 1) * columns] = low[v * depth:(v + 1) * depth]
            mid_cat[start + 2 * depth:start + 3 * depth, v * columns:(v + 1) * columns] = high[v * depth:(v + 1) * depth]
    left_copy.wait()
    total = jnp.dot(left_in[...], mid_cat[...], preferred_element_type=jnp.float32)
    half = len(order) // 2
    for v in range(count):
        for p in range(len(order)):
            ref = sent if p < half else kept
            ref[p % half, v] = total[p * piece:(p + 1) * piece, v * columns:(v + 1) * columns]


def chunk(scalars, left_cat, rights, psis, halos, first, count, order, earlier=()):
    rows = left_cat.shape[1]
    depth, width = psis[0].shape[2:]
    terms, columns = rights[0].shape[0], rights[0].shape[3] // 2
    with_halo = len(halos or ())
    args = [left_cat] + pinned(pltpu.HBM, rights[0]) + [rights[1]] + pinned(pltpu.HBM, psis[0]) + [psis[1], *(halos or ()), *earlier]
    out = jax.ShapeDtypeStruct((len(order) // 2, count, rows // len(order), columns), jnp.float32)
    flops = 2 * 3 * terms * count * rows * columns * (depth + 2 * width)
    sources = 2 + (with_halo > 0)
    return pl.pallas_call(
        functools.partial(chunk_kernel, order, terms, first, count, with_halo),
        out_shape=(out, out),
        in_specs=[pl.BlockSpec(memory_space=pltpu.SMEM)] + [ANY] * len(args),
        out_specs=(VMEM,) * 2,
        scratch_shapes=[
            pltpu.VMEM((rows, terms * 3 * depth), jnp.bfloat16),
            pltpu.VMEM((2, terms, width, columns), jnp.float32),
            pltpu.VMEM((sources, 2, count, depth, width), jnp.float32),
            pltpu.VMEM((terms, 4 * width, 2 * columns), jnp.bfloat16),
            pltpu.VMEM((sources, count * depth, 4 * width), jnp.bfloat16),
            pltpu.VMEM((terms * 3 * depth, count * columns), jnp.bfloat16),
            pltpu.SemaphoreType.DMA((3 + 2 * sources + with_halo,)),
        ],
        compiler_params=pltpu.CompilerParams(vmem_limit_bytes=20 * 1024 * 1024),
        cost_estimate=pl.CostEstimate(flops=1024, bytes_accessed=1024, transcendentals=0),
        name="terms_of_sector",
    )(scalars, *args)


def shards(wavefunction, left_operators, right_operators, source_sectors):
    sectors, vectors = wavefunction.shape[:2]
    assert sectors == 2
    peers, places = lax.axis_size("term"), lax.axis_size("sec")
    z, x, core = lax.axis_index("term"), lax.axis_index("sec"), lax.axis_index("sub")
    order = halving_order(peers)
    stages = [[(i, i ^ (1 << b)) for i in range(peers)] for b in range(peers.bit_length() - 1)]
    swap = [(0, 1), (1, 0)]
    relative = source_sectors - x * sectors
    picks = jnp.where((relative >= 0) & (relative < sectors), relative, 2)
    count = vectors // 2
    psis = [wavefunction, lax.ppermute(wavefunction, "sub", swap)]
    rights = [right_operators, lax.ppermute(right_operators, "sub", swap)]
    left_cat = None

    targets = (x, 1 - x) if places == 2 else (jnp.int32(0), jnp.int32(1))

    if places == 2:
        ways = [None, (targets[1], swap)]
    else:
        up = [(i, i + 1) for i in range(places - 1)]
        ways = [(jnp.int32(1), up), (jnp.int32(0), [(j, i) for i, j in up])]
    halos = {}
    for which in range(2):
        if ways[which] is not None:
            for first in range(0, vectors, count):
                edge = edge_of(ways[which][0], wavefunction, first, count, *([] if left_cat is None else [left_cat]))
                halos[which, first] = lax.ppermute(edge, "sec", ways[which][1])
                if left_cat is None:
                    left_cat = staged(z, left_operators, order, edge)

    def compute(item, earlier, tie):
        which, first, count = item
        sources = lax.dynamic_index_in_dim(picks, targets[which], 1, keepdims=False)
        both = None
        if (which, first) in halos:
            halo = relay(halos[which, first], *tie) if tie is not None else halos[which, first]
            both = [halo] + [lax.ppermute(halo[v:v + 1], "sub", swap) for v in range(0, count, 1)]
        else:
            sources = jnp.minimum(sources, 1)
        scalars = jnp.concatenate([jnp.stack([targets[which], core]), sources])
        return chunk(scalars, left_cat, rights, psis, both, first, count, order, earlier)

    work = [(which, first, count) for which in range(2) for first in range(0, vectors, count)]
    parts = {}

    def begin(item, earlier=(), tie=None):
        sent, kept = compute(item, list(earlier), tie)
        parts[item] = [(kept, 0), (lax.ppermute(sent, "term", stages[0]), 0)]
        return sent

    def proceed(item, stage, earlier=()):
        half = peers >> (stage + 1)
        sent = summed(parts[item], half, list(earlier))
        parts[item] = [(array, start + half) for array, start in parts[item]]
        parts[item].append((lax.ppermute(sent, "term", stages[stage]), 0))
        return sent

    late = range(1, len(stages))
    a1, a2, b1, b2 = work
    sent = begin(a1)
    sent = begin(a2)
    last = [proceed(a1, stage, [sent]) for stage in late][-1]
    sent = begin(b1, tie=[last])
    last = [proceed(a2, stage, [sent]) for stage in late][-1]
    sent = begin(b2, [parts[a1][-1][0]], tie=[last])
    for stage in late:
        proceed(b1, stage, [sent])
    for stage in late:
        proceed(b2, stage)
    out = gathered(targets, {item: parts[item] for item in (a1, a2, b1)}, (sectors, vectors) + parts[a1][0][0].shape[2:])
    total = sum(array[start:start + 1] for array, start in parts[b2])
    return lax.dynamic_update_slice(out, total, (targets[1], b2[1], 0, 0))


def solution(mesh):
    in_specs = (
        P(("grp", "sec"), None, None, "sub"),
        P("term", ("grp", "sec"), None, None),
        P("term", ("grp", "sec"), "sub", None),
        P("term", ("grp", "sec")),
    )
    out_specs = P(("grp", "sec"), None, "term", "sub")
    return jax.shard_map(shards, mesh=mesh, in_specs=in_specs, out_specs=out_specs, check_vma=False)
```
